32 devices in a mesh: head: 4 (over y, core), seq: 8 (over z, x).
Axes of the slice: x: 2, y: 2, z: 4, core: 2. Of those that a mesh axis runs over, the one named last changes fastest.
Arguments:
- query_rows: bfloat16 [8192, 1024], P(('seq', 'head')), may hold values from -0.5 to 0.5
- key_rows: bfloat16 [8192, 1024], P(('seq', 'head')), may hold values from -0.5 to 0.5
- value_rows: bfloat16 [8192, 1024], P(('seq', 'head')), may hold values from -0.5 to 0.5
- grad_rows: bfloat16 [8192, 1024], P(('seq', 'head')), may hold values from -0.5 to 0.5
Outputs:
- attended: bfloat16 [8192, 1024], P(('seq', 'head'))
- grad_query: bfloat16 [8192, 1024], P(('seq', 'head'))
- grad_key: bfloat16 [8192, 1024], P(('seq', 'head'))
- grad_value: bfloat16 [8192, 1024], P(('seq', 'head'))
The draws below stay inside these ranges and needn't reach their ends.
All inputs are finite; a program needn't handle non-finite values.
Results may differ from the reference program's by a relative error of at most 0.0051.
Values may be sent and summed in bfloat16 or wider, within the bound.
A program may use at most 64 MiB of HBM per device.

```python
import jax
import jax.numpy as jnp
from jax import lax

HEAD_DIM = 128
TOK_SEQ = 1024
HEADS = 8
TOKENS = 8192
N_SEQ = 8


def levels(own_key, shape, split, low, top_value):
    def one(axis_at, blocks):
        draws = jax.random.uniform(jax.random.fold_in(jax.random.fold_in(own_key, 6), axis_at), (blocks,), jnp.float32, low / len(split), top_value / len(split))
        return jnp.repeat(jnp.exp(draws), shape[axis_at] // blocks).reshape((-1,) + (1,) * (len(shape) - axis_at - 1))

    level = one(*split[0])
    for cut in split[1:]:
        level = level * one(*cut)
    return level


def normal_values(stream_key, shape, scale, bound, split=(), kind=jnp.bfloat16):
    values = scale * jax.random.normal(stream_key, shape, jnp.float32)
    if split:
        values = values * levels(stream_key, shape, split, -0.22, 0.18)
    return jnp.clip(values, -bound, bound).astype(kind)


def setup_inputs(seed: int = 0) -> dict:
    arg_keys = jax.random.split(jax.random.key(seed), 5)
    query_rows = normal_values(arg_keys[0], (TOKENS, HEADS * HEAD_DIM), 0.08, 0.5, ((0, 32),))
    key_rows = normal_values(arg_keys[1], (TOKENS, HEADS * HEAD_DIM), 0.08, 0.5, ((0, 32),))
    value_rows = normal_values(arg_keys[2], (TOKENS, HEADS * HEAD_DIM), 0.08, 0.5, ((0, 32),))
    grad_rows = normal_values(arg_keys[3], (TOKENS, HEADS * HEAD_DIM), 0.08, 0.5, ((0, 32),))
    return dict(query_rows=query_rows, key_rows=key_rows, value_rows=value_rows, grad_rows=grad_rows)


def to_blocks(rows):
    shaped = rows.reshape(N_SEQ, TOK_SEQ, HEADS, HEAD_DIM)
    return jnp.transpose(shaped, (2, 0, 1, 3))


def from_blocks(blocks):
    return jnp.transpose(blocks, (1, 2, 0, 3)).reshape(N_SEQ * TOK_SEQ, HEADS * HEAD_DIM)


def one_head(items):
    query, keyset, valueset, cograd = items
    qf = query.astype(jnp.float32)
    kf = keyset.astype(jnp.float32)
    vf = valueset.astype(jnp.float32)
    gf = cograd.astype(jnp.float32)
    state = jnp.einsum('btd,bte->bde', kf, vf)
    qgrad = jnp.einsum('btd,bte->bde', qf, gf)
    zero = jnp.zeros((1, HEAD_DIM, HEAD_DIM), jnp.float32)
    prefix = jnp.concatenate([zero, jnp.cumsum(state, axis=0)[:-1]], axis=0)
    suffix = jnp.concatenate([jnp.cumsum(qgrad[::-1], axis=0)[:-1][::-1], zero], axis=0)
    prefix16 = prefix.astype(jnp.bfloat16).astype(jnp.float32)
    suffix16 = suffix.astype(jnp.bfloat16).astype(jnp.float32)
    rowpos = lax.broadcasted_iota(jnp.int32, (TOK_SEQ, TOK_SEQ), 0)
    colpos = lax.broadcasted_iota(jnp.int32, (TOK_SEQ, TOK_SEQ), 1)
    causal = (colpos <= rowpos)[None]
    scores = jnp.where(causal, jnp.einsum('btd,bsd->bts', qf, kf), 0.0).astype(jnp.bfloat16).astype(jnp.float32)
    attended = jnp.einsum('bts,bsd->btd', scores, vf) + jnp.einsum('btd,bde->bte', qf, prefix16)
    dprob = jnp.where(causal, jnp.einsum('btd,bsd->bts', gf, vf), 0.0).astype(jnp.bfloat16).astype(jnp.float32)
    grad_query = jnp.einsum('bts,bsd->btd', dprob, kf) + jnp.einsum('btd,bed->bte', gf, prefix16)
    grad_key = jnp.einsum('bts,btd->bsd', dprob, qf) + jnp.einsum('bse,bde->bsd', vf, suffix16)
    grad_value = jnp.einsum('bts,bte->bse', scores, gf) + jnp.einsum('bsd,bde->bse', kf, suffix16)
    return (attended.astype(jnp.bfloat16), grad_query.astype(jnp.bfloat16),
            grad_key.astype(jnp.bfloat16), grad_value.astype(jnp.bfloat16))


def reference(query_rows, key_rows, value_rows, grad_rows):
    items = (to_blocks(query_rows), to_blocks(key_rows), to_blocks(value_rows), to_blocks(grad_rows))
    attended, grad_query, grad_key, grad_value = lax.map(one_head, items)
    return (from_blocks(attended), from_blocks(grad_query), from_blocks(grad_key), from_blocks(grad_value))
```

```python
import functools

import jax
import jax.numpy as jnp
from jax import lax
from jax.experimental import pallas as pl
from jax.experimental.pallas import tpu as pltpu
from jax.sharding import PartitionSpec as P

HEAD_DIM = 128
MESH = pl.DeviceIdType.MESH


def dot(a, b, ca, cb):
    return lax.dot_general(a, b, (((ca,), (cb,)), ((), ())), preferred_element_type=jnp.float32)


def kernel(nh, ns, nx, q_ref, k_ref, v_ref, g_ref, o_ref, gq_ref, gk_ref, gv_ref,
           part, got, zpart, zgot, back, pre, acc,
           send1, recv1, send3, recv3, send4, recv4):
    tokens, width = q_ref.shape
    heads = width // HEAD_DIM
    group = nh * nx
    planes = ns // nx
    rows = width // group
    head_at, seq_at = lax.axis_index("head"), lax.axis_index("seq")
    z, me = seq_at // nx, lax.rem(seq_at, nx) * nh + head_at

    def in_plane(p):
        return {"head": lax.rem(p, nh), "seq": z * nx + p // nh}

    def in_column(zz):
        return {"head": head_at, "seq": zz * nx + lax.rem(seq_at, nx)}

    def rows_of(p):
        start = p * rows
        return pl.ds(start if isinstance(start, int) else pl.multiple_of(start, rows), rows)

    barrier = pltpu.get_barrier_semaphore()
    for k in range(1, group):
        pl.semaphore_signal(barrier, inc=1, device_id=in_plane(lax.rem(me + k, group)), device_id_type=MESH)
    for k in range(1, planes):
        pl.semaphore_signal(barrier, inc=1, device_id=in_column(lax.rem(z + k, planes)), device_id_type=MESH)

    for h in range(heads):
        cols = slice(h * HEAD_DIM, (h + 1) * HEAD_DIM)
        part[0, cols, :] = dot(k_ref[:, cols], v_ref[:, cols], 0, 0).astype(part.dtype)
        part[1, cols, :] = dot(q_ref[:, cols], g_ref[:, cols], 0, 0).astype(part.dtype)

    pl.semaphore_wait(barrier, group + planes - 2)

    def copy1(dst_p, slot):
        return pltpu.make_async_remote_copy(
            src_ref=part.at[:, rows_of(dst_p), :], dst_ref=got.at[slot],
            send_sem=send1.at[dst_p], recv_sem=recv1.at[slot],
            device_id=in_plane(dst_p), device_id_type=MESH)

    for k in range(1, group):
        copy1(lax.rem(me + k, group), me).start()
    got[me] = part[:, rows_of(me), :]

    causal = (lax.broadcasted_iota(jnp.int32, (tokens, tokens), 1)
              <= lax.broadcasted_iota(jnp.int32, (tokens, tokens), 0))
    for h in range(heads):
        cols = slice(h * HEAD_DIM, (h + 1) * HEAD_DIM)
        q, kk, v, g = q_ref[:, cols], k_ref[:, cols], v_ref[:, cols], g_ref[:, cols]
        scores = jnp.where(causal, dot(q, kk, 1, 1), 0.0).astype(jnp.bfloat16)
        dprob = jnp.where(causal, dot(g, v, 1, 1), 0.0).astype(jnp.bfloat16)
        acc[0, :, cols] = dot(scores, v, 1, 0)
        acc[1, :, cols] = dot(dprob, kk, 1, 0)
        acc[2, :, cols] = dot(dprob, q, 0, 0)
        acc[3, :, cols] = dot(scores, g, 0, 0)

    for k in range(1, group):
        source = lax.rem(me + group - k, group)
        copy1(source, source).wait_recv()

    total = got[0].astype(jnp.float32)
    for p in range(1, group):
        total = total + got[p].astype(jnp.float32)
    zpart[...] = total.astype(zpart.dtype)

    def copy3(which, zz, slot):
        return pltpu.make_async_remote_copy(
            src_ref=zpart.at[which], dst_ref=zgot.at[which, slot],
            send_sem=send3.at[which, zz], recv_sem=recv3.at[which, slot],
            device_id=in_column(zz), device_id_type=MESH)

    for zz in range(planes):
        @pl.when(zz > z)
        def _():
            copy3(0, zz, z).start()

        @pl.when(zz < z)
        def _():
            copy3(1, zz, z).start()

    for zz in range(planes):
        @pl.when(zz >= z)
        def _():
            zgot[0, zz] = jnp.zeros(zgot.shape[2:], zgot.dtype)

        @pl.when(zz <= z)
        def _():
            zgot[1, zz] = jnp.zeros(zgot.shape[2:], zgot.dtype)

    for zz in range(planes):
        @pl.when(zz < z)
        def _():
            copy3(0, zz, zz).wait_recv()

        @pl.when(zz > z)
        def _():
            copy3(1, zz, zz).wait_recv()

    run = zgot[0, 0].astype(jnp.float32)
    for zz in range(1, planes):
        run = run + zgot[0, zz].astype(jnp.float32)
    for p in range(group):
        back[p, 0] = run.astype(jnp.bfloat16)
        if p < group - 1:
            run = run + got[p, 0].astype(jnp.float32)
    run = zgot[1, 0].astype(jnp.float32)
    for zz in range(1, planes):
        run = run + zgot[1, zz].astype(jnp.float32)
    for p in range(group - 1, -1, -1):
        back[p, 1] = run.astype(jnp.bfloat16)
        if p > 0:
            run = run + got[p, 1].astype(jnp.float32)

    def copy4(dst_p, owner):
        return pltpu.make_async_remote_copy(
            src_ref=back.at[dst_p], dst_ref=pre.at[:, rows_of(owner), :],
            send_sem=send4.at[dst_p], recv_sem=recv4.at[owner],
            device_id=in_plane(dst_p), device_id_type=MESH)

    for k in range(1, group):
        copy4(lax.rem(me + k, group), me).start()
    pre[:, rows_of(me), :] = back[me]
    for k in range(1, group):
        source = lax.rem(me + group - k, group)
        copy4(source, source).wait_recv()

    for h in range(heads):
        cols = slice(h * HEAD_DIM, (h + 1) * HEAD_DIM)
        q, kk, v, g = q_ref[:, cols], k_ref[:, cols], v_ref[:, cols], g_ref[:, cols]
        prefix, suffix = pre[0, cols, :], pre[1, cols, :]
        o_ref[:, cols] = (acc[0, :, cols] + dot(q, prefix, 1, 0)).astype(jnp.bfloat16)
        gq_ref[:, cols] = (acc[1, :, cols] + dot(g, prefix, 1, 1)).astype(jnp.bfloat16)
        gk_ref[:, cols] = (acc[2, :, cols] + dot(v, suffix, 1, 1)).astype(jnp.bfloat16)
        gv_ref[:, cols] = (acc[3, :, cols] + dot(kk, suffix, 1, 0)).astype(jnp.bfloat16)

    for k in range(1, group):
        there = lax.rem(me + k, group)
        copy1(there, me).wait_send()
        copy4(there, me).wait_send()
    for zz in range(planes):
        @pl.when(zz > z)
        def _():
            copy3(0, zz, z).wait_send()

        @pl.when(zz < z)
        def _():
            copy3(1, zz, z).wait_send()


def per_device(nh, ns, query_rows, key_rows, value_rows, grad_rows):
    tokens, width = query_rows.shape
    nx = 1
    while 2 * (2 * nx) ** 2 <= ns and ns % (2 * nx) == 0:
        nx *= 2
    group, planes = nh * nx, ns // nx
    rows = width // group
    bf16, f32 = jnp.bfloat16, jnp.float32
    vmem = pl.BlockSpec(memory_space=pltpu.VMEM)
    return pl.pallas_call(
        functools.partial(kernel, nh, ns, nx),
        out_shape=(jax.ShapeDtypeStruct((tokens, width), bf16),) * 4,
        in_specs=[vmem] * 4,
        out_specs=(vmem,) * 4,
        scratch_shapes=[
            pltpu.VMEM((2, width, HEAD_DIM), bf16),
            pltpu.VMEM((group, 2, rows, HEAD_DIM), bf16),
            pltpu.VMEM((2, rows, HEAD_DIM), bf16),
            pltpu.VMEM((2, planes, rows, HEAD_DIM), bf16),
            pltpu.VMEM((group, 2, rows, HEAD_DIM), bf16),
            pltpu.VMEM((2, width, HEAD_DIM), bf16),
            pltpu.VMEM((4, tokens, width), f32),
            pltpu.SemaphoreType.DMA((group,)),
            pltpu.SemaphoreType.DMA((group,)),
            pltpu.SemaphoreType.DMA((2, planes)),
            pltpu.SemaphoreType.DMA((2, planes)),
            pltpu.SemaphoreType.DMA((group,)),
            pltpu.SemaphoreType.DMA((group,)),
        ],
        compiler_params=pltpu.CompilerParams(
            collective_id=0, has_side_effects=True, vmem_limit_bytes=48 * 1024 * 1024),
        cost_estimate=pl.CostEstimate(
            flops=tokens * width * (8 * tokens + 12 * HEAD_DIM),
            bytes_accessed=16 * tokens * width, transcendentals=0),
    )(query_rows, key_rows, value_rows, grad_rows)


def solution(mesh):
    placed = P(("seq", "head"), None)
    return jax.shard_map(
        functools.partial(per_device, mesh.shape["head"], mesh.shape["seq"]),
        mesh=mesh,
        in_specs=(placed,) * 4,
        out_specs=(placed,) * 4,
        check_vma=False,
    )
```

```python
import functools

import jax
import jax.numpy as jnp
from jax import lax
from jax.experimental import pallas as pl
from jax.experimental.pallas import tpu as pltpu
from jax.sharding import PartitionSpec as P

HEAD_DIM = 128
CORES = 2
MESH = pl.DeviceIdType.MESH


def dot(a, b, ca, cb):
    return lax.dot_general(a, b, (((ca,), (cb,)), ((), ())), preferred_element_type=jnp.float32)


def states_kernel(nh, ns, nx, q_hbm, k_hbm, v_hbm, g_hbm, o_ref, gq_ref, gk_ref, gv_ref,
                  q_ref, k_ref, v_ref, g_ref, other, paired, own, chip, got, zpart, zgot,
                  back, chippre, mate, pre, acc,
                  in_sem, send0, recv0, send1, recv1, send2, recv2, send3, recv3, send4, recv4):
    tokens, width = q_ref.shape
    heads = width // HEAD_DIM
    half = heads // CORES
    along = nh // CORES
    chips = along * nx
    planes = ns // nx
    half_rows = half * HEAD_DIM
    rows = half_rows // chips
    head_at, seq_at = lax.axis_index("head"), lax.axis_index("seq")
    core = lax.rem(head_at, CORES)
    z = seq_at // nx
    me = lax.rem(seq_at, nx) * along + head_at // CORES
    first, mine = core * half, (1 - core) * half
    partner = {"head": head_at + 1 - 2 * core, "seq": seq_at}

    def in_plane(p):
        return {"head": lax.rem(p, along) * CORES + core, "seq": z * nx + p // along}

    def in_column(zz):
        return {"head": head_at, "seq": zz * nx + lax.rem(seq_at, nx)}

    def rows_of(p):
        return pl.ds(pl.multiple_of(p * rows, rows), rows)

    def cols_of(h):
        return pl.ds(pl.multiple_of(h * HEAD_DIM, HEAD_DIM), HEAD_DIM)

    loads = [pltpu.make_async_copy(src, dst, in_sem.at[i]) for i, (src, dst) in enumerate(
        ((k_hbm, k_ref), (v_hbm, v_ref), (q_hbm, q_ref), (g_hbm, g_ref)))]
    for load in loads:
        load.start()

    barrier = pltpu.get_barrier_semaphore()
    pl.semaphore_signal(barrier, inc=1, device_id=partner, device_id_type=MESH)
    for k in range(1, chips):
        pl.semaphore_signal(barrier, inc=1, device_id=in_plane(lax.rem(me + k, chips)), device_id_type=MESH)
    for k in range(1, planes):
        pl.semaphore_signal(barrier, inc=1, device_id=in_column(lax.rem(z + k, planes)), device_id_type=MESH)

    def copy0(a):
        return pltpu.make_async_remote_copy(
            src_ref=other.at[a], dst_ref=paired.at[a], send_sem=send0.at[a], recv_sem=recv0.at[a],
            device_id=partner, device_id_type=MESH)

    def copy1(a, there, slot):
        return pltpu.make_async_remote_copy(
            src_ref=chip.at[a, rows_of(there), :], dst_ref=got.at[slot, a],
            send_sem=send1.at[a, there], recv_sem=recv1.at[a, slot],
            device_id=in_plane(there), device_id_type=MESH)

    def copy2(a, zz, slot):
        return pltpu.make_async_remote_copy(
            src_ref=zpart.at[a], dst_ref=zgot.at[a, slot],
            send_sem=send2.at[a, zz], recv_sem=recv2.at[a, slot],
            device_id=in_column(zz), device_id_type=MESH)

    def copy3(a, there, owner):
        return pltpu.make_async_remote_copy(
            src_ref=back.at[there, a], dst_ref=chippre.at[a, rows_of(owner), :],
            send_sem=send3.at[a, there], recv_sem=recv3.at[a, owner],
            device_id=in_plane(there), device_id_type=MESH)

    def copy4(a, whose):
        return pltpu.make_async_remote_copy(
            src_ref=mate.at[a],
            dst_ref=pre.at[a, pl.ds(pl.multiple_of(whose * half_rows, half_rows), half_rows), :],
            send_sem=send4.at[a], recv_sem=recv4.at[a], device_id=partner, device_id_type=MESH)

    for a, (x_ref, y_ref) in enumerate(((k_ref, v_ref), (q_ref, g_ref))):
        loads[2 * a].wait()
        loads[2 * a + 1].wait()
        for h in range(half):
            cols, at = cols_of(mine + h), slice(h * HEAD_DIM, (h + 1) * HEAD_DIM)
            other[a, at, :] = dot(x_ref[:, cols], y_ref[:, cols], 0, 0).astype(other.dtype)
        if a == 0:
            pl.semaphore_wait(barrier, chips + planes - 1)
        copy0(a).start()
        for h in range(half):
            cols, at = cols_of(first + h), slice(h * HEAD_DIM, (h + 1) * HEAD_DIM)
            own[a, at, :] = dot(x_ref[:, cols], y_ref[:, cols], 0, 0)

    for a in range(2):
        copy0(a).wait_recv()
        chip[a] = (own[a] + paired[a].astype(jnp.float32)).astype(chip.dtype)
        for k in range(1, chips):
            copy1(a, lax.rem(me + k, chips), me).start()
        got[me, a] = chip[a, rows_of(me), :]

    causal = (lax.broadcasted_iota(jnp.int32, (tokens, tokens), 1)
              <= lax.broadcasted_iota(jnp.int32, (tokens, tokens), 0))

    def within(begin, end):
        for h in range(begin, end):
            cols = slice(h * HEAD_DIM, (h + 1) * HEAD_DIM)
            q, kk, v, g = q_ref[:, cols], k_ref[:, cols], v_ref[:, cols], g_ref[:, cols]
            scores = jnp.where(causal, dot(q, kk, 1, 1), 0.0).astype(jnp.bfloat16)
            dprob = jnp.where(causal, dot(g, v, 1, 1), 0.0).astype(jnp.bfloat16)
            acc[0, :, cols] = dot(scores, v, 1, 0)
            acc[1, :, cols] = dot(dprob, kk, 1, 0)
            acc[2, :, cols] = dot(dprob, q, 0, 0)
            acc[3, :, cols] = dot(scores, g, 0, 0)

    cut1, cut2 = heads * 3 // 8, heads * 5 // 8
    within(0, cut1)

    for a in range(2):
        for k in range(1, chips):
            source = lax.rem(me + chips - k, chips)
            copy1(a, source, source).wait_recv()
        total = got[0, a].astype(jnp.float32)
        for p in range(1, chips):
            total = total + got[p, a].astype(jnp.float32)
        zpart[a] = total.astype(zpart.dtype)
        for zz in range(planes):
            @pl.when(zz > z if a == 0 else zz < z)
            def _():
                copy2(a, zz, z).start()

    for a in range(2):
        for zz in range(planes):
            @pl.when(zz >= z if a == 0 else zz <= z)
            def _():
                zgot[a, zz] = jnp.zeros(zgot.shape[2:], zgot.dtype)

    within(cut1, cut2)

    for a in range(2):
        for zz in range(planes):
            @pl.when(zz < z if a == 0 else zz > z)
            def _():
                copy2(a, zz, zz).wait_recv()
        run = zgot[a, 0].astype(jnp.float32)
        for zz in range(1, planes):
            run = run + zgot[a, zz].astype(jnp.float32)
        order = range(chips) if a == 0 else range(chips - 1, -1, -1)
        for p in order:
            back[p, a] = run.astype(jnp.bfloat16)
            run = run + got[p, a].astype(jnp.float32)
        for k in range(1, chips):
            copy3(a, lax.rem(me + k, chips), me).start()
        chippre[a, rows_of(me), :] = back[me, a]

    within(cut2, heads)

    my_rows = pl.ds(pl.multiple_of(core * half_rows, half_rows), half_rows)
    for a in range(2):
        for k in range(1, chips):
            source = lax.rem(me + chips - k, chips)
            copy3(a, source, source).wait_recv()
        base = chippre[a].astype(jnp.float32)
        later = core == (1 if a == 0 else 0)
        mate[a] = (base + jnp.where(later, 0.0, own[a])).astype(jnp.bfloat16)
        copy4(a, core).start()
        pre[a, my_rows, :] = (base + jnp.where(later, paired[a].astype(jnp.float32), 0.0)).astype(jnp.bfloat16)

    def finish(start):
        for h in range(half):
            cols = cols_of(start + h)
            q, kk, v, g = q_ref[:, cols], k_ref[:, cols], v_ref[:, cols], g_ref[:, cols]
            prefix, suffix = pre[0, cols, :], pre[1, cols, :]
            o_ref[:, cols] = (acc[0, :, cols] + dot(q, prefix, 1, 0)).astype(jnp.bfloat16)
            gq_ref[:, cols] = (acc[1, :, cols] + dot(g, prefix, 1, 1)).astype(jnp.bfloat16)
            gk_ref[:, cols] = (acc[2, :, cols] + dot(v, suffix, 1, 1)).astype(jnp.bfloat16)
            gv_ref[:, cols] = (acc[3, :, cols] + dot(kk, suffix, 1, 0)).astype(jnp.bfloat16)

    finish(first)
    for a in range(2):
        copy4(a, 1 - core).wait_recv()
    finish(mine)

    for a in range(2):
        copy0(a).wait_send()
        copy4(a, core).wait_send()
        for k in range(1, chips):
            there = lax.rem(me + k, chips)
            copy1(a, there, me).wait_send()
            copy3(a, there, me).wait_send()
        for zz in range(planes):
            @pl.when(zz > z if a == 0 else zz < z)
            def _():
                copy2(a, zz, z).wait_send()


def store_kernel(*refs):
    sources, targets, sem = refs[:4], refs[4:8], refs[8]
    copies = [pltpu.make_async_copy(s, t, sem.at[i]) for i, (s, t) in enumerate(zip(sources, targets))]
    for copy in copies:
        copy.start()
    for copy in copies:
        copy.wait()


def per_device(nh, ns, query_rows, key_rows, value_rows, grad_rows):
    tokens, width = query_rows.shape
    nx = 1
    while 2 * (2 * nx) ** 2 <= ns and ns % (2 * nx) == 0:
        nx *= 2
    chips, planes = nh // CORES * nx, ns // nx
    half_rows = width // CORES
    rows = half_rows // chips
    bf16, f32 = jnp.bfloat16, jnp.float32
    vmem, hbm = pl.BlockSpec(memory_space=pltpu.VMEM), pl.BlockSpec(memory_space=pltpu.HBM)
    dma = pltpu.SemaphoreType.DMA
    shape = (jax.ShapeDtypeStruct((tokens, width), bf16),) * 4
    results = pl.pallas_call(
        functools.partial(states_kernel, nh, ns, nx),
        out_shape=shape,
        in_specs=[hbm] * 4,
        out_specs=(vmem,) * 4,
        scratch_shapes=[pltpu.VMEM((tokens, width), bf16)] * 4 + [
            pltpu.VMEM((2, half_rows, HEAD_DIM), f32),
            pltpu.VMEM((2, half_rows, HEAD_DIM), f32),
            pltpu.VMEM((2, half_rows, HEAD_DIM), f32),
            pltpu.VMEM((2, half_rows, HEAD_DIM), bf16),
            pltpu.VMEM((chips, 2, rows, HEAD_DIM), bf16),
            pltpu.VMEM((2, rows, HEAD_DIM), bf16),
            pltpu.VMEM((2, planes, rows, HEAD_DIM), bf16),
            pltpu.VMEM((chips, 2, rows, HEAD_DIM), bf16),
            pltpu.VMEM((2, half_rows, HEAD_DIM), bf16),
            pltpu.VMEM((2, half_rows, HEAD_DIM), bf16),
            pltpu.VMEM((2, width, HEAD_DIM), bf16),
            pltpu.VMEM((4, tokens, width), f32),
            dma((4,)), dma((2,)), dma((2,)), dma((2, chips)), dma((2, chips)),
            dma((2, planes)), dma((2, planes)), dma((2, chips)), dma((2, chips)), dma((2,)), dma((2,)),
        ],
        compiler_params=pltpu.CompilerParams(
            collective_id=0, has_side_effects=True, vmem_limit_bytes=103 * 512 * 1024),
        cost_estimate=pl.CostEstimate(
            flops=tokens * width * (8 * tokens + 12 * HEAD_DIM),
            bytes_accessed=16 * tokens * width, transcendentals=0),
    )(query_rows, key_rows, value_rows, grad_rows)
    return pl.pallas_call(
        store_kernel,
        out_shape=shape,
        in_specs=[vmem] * 4,
        out_specs=(hbm,) * 4,
        scratch_shapes=[dma((4,))],
        compiler_params=pltpu.CompilerParams(vmem_limit_bytes=8 * 1024 * 1024),
        cost_estimate=pl.CostEstimate(flops=0, bytes_accessed=16 * tokens * width, transcendentals=0),
    )(*results)


def solution(mesh):
    placed = P(("seq", "head"), None)
    return jax.shard_map(
        functools.partial(per_device, mesh.shape["head"], mesh.shape["seq"]),
        mesh=mesh,
        in_specs=(placed,) * 4,
        out_specs=(placed,) * 4,
        check_vma=False,
    )
```

```python
import functools

import jax
import jax.numpy as jnp
from jax import lax
from jax.experimental import pallas as pl
from jax.experimental.pallas import tpu as pltpu
from jax.sharding import PartitionSpec as P

HEAD_DIM = 128
CORES = 2
MESH = pl.DeviceIdType.MESH


def dot(a, b, ca, cb):
    return lax.dot_general(a, b, (((ca,), (cb,)), ((), ())), preferred_element_type=jnp.float32)


def states_kernel(nh, ns, nx, q_hbm, k_hbm, v_hbm, g_hbm, o_ref, gq_ref, gk_ref, gv_ref,
                  q_ref, k_ref, v_ref, g_ref, other, paired, own, chip, got, zpart, zgot,
                  back, chippre, mate, pre, acc,
                  in_sem, send0, recv0, send1, recv1, send2, recv2, send3, recv3, send4, recv4):
    tokens, width = q_ref.shape
    heads = width // HEAD_DIM
    half = heads // CORES
    along = nh // CORES
    chips = along * nx
    planes = ns // nx
    half_rows = half * HEAD_DIM
    rows = half_rows // chips
    head_at, seq_at = lax.axis_index("head"), lax.axis_index("seq")
    core = lax.rem(head_at, CORES)
    z = seq_at // nx
    me = lax.rem(seq_at, nx) * along + head_at // CORES
    first, mine = core * half, (1 - core) * half
    partner = {"head": head_at + 1 - 2 * core, "seq": seq_at}

    def in_plane(p):
        return {"head": lax.rem(p, along) * CORES + core, "seq": z * nx + p // along}

    def in_column(zz):
        return {"head": head_at, "seq": zz * nx + lax.rem(seq_at, nx)}

    def rows_of(p):
        return pl.ds(pl.multiple_of(p * rows, rows), rows)

    def cols_of(h):
        return pl.ds(pl.multiple_of(h * HEAD_DIM, HEAD_DIM), HEAD_DIM)

    loads = [pltpu.make_async_copy(src, dst, in_sem.at[i]) for i, (src, dst) in enumerate(
        ((k_hbm, k_ref), (v_hbm, v_ref), (q_hbm, q_ref), (g_hbm, g_ref)))]
    for load in loads:
        load.start()

    barrier = pltpu.get_barrier_semaphore()
    pl.semaphore_signal(barrier, inc=1, device_id=partner, device_id_type=MESH)
    for k in range(1, chips):
        pl.semaphore_signal(barrier, inc=1, device_id=in_plane(lax.rem(me + k, chips)), device_id_type=MESH)
    for k in range(1, planes):
        pl.semaphore_signal(barrier, inc=1, device_id=in_column(lax.rem(z + k, planes)), device_id_type=MESH)

    def copy0(a):
        return pltpu.make_async_remote_copy(
            src_ref=other.at[a], dst_ref=paired.at[a], send_sem=send0.at[a], recv_sem=recv0.at[a],
            device_id=partner, device_id_type=MESH)

    def copy1(a, there, slot):
        return pltpu.make_async_remote_copy(
            src_ref=chip.at[a, rows_of(there), :], dst_ref=got.at[slot, a],
            send_sem=send1.at[a, there], recv_sem=recv1.at[a, slot],
            device_id=in_plane(there), device_id_type=MESH)

    def copy2(a, zz, slot):
        return pltpu.make_async_remote_copy(
            src_ref=zpart.at[a], dst_ref=zgot.at[a, slot],
            send_sem=send2.at[a, zz], recv_sem=recv2.at[a, slot],
            device_id=in_column(zz), device_id_type=MESH)

    def copy3(a, there, owner):
        return pltpu.make_async_remote_copy(
            src_ref=back.at[there, a], dst_ref=chippre.at[a, rows_of(owner), :],
            send_sem=send3.at[a, there], recv_sem=recv3.at[a, owner],
            device_id=in_plane(there), device_id_type=MESH)

    def copy4(a, whose):
        return pltpu.make_async_remote_copy(
            src_ref=mate.at[a],
            dst_ref=pre.at[a, pl.ds(pl.multiple_of(whose * half_rows, half_rows), half_rows), :],
            send_sem=send4.at[a], recv_sem=recv4.at[a], device_id=partner, device_id_type=MESH)

    def states_of(a, start, out):
        x_ref, y_ref = ((k_ref, v_ref), (q_ref, g_ref))[a]
        for h in range(half):
            cols, at = cols_of(start + h), slice(h * HEAD_DIM, (h + 1) * HEAD_DIM)
            out[a, at, :] = dot(x_ref[:, cols], y_ref[:, cols], 0, 0)

    def chip_sums(a):
        copy0(a).wait_recv()
        chip[a] = (own[a] + paired[a]).astype(chip.dtype)
        for k in range(1, chips):
            copy1(a, lax.rem(me + k, chips), me).start()
        got[me, a] = chip[a, rows_of(me), :]

    loads[0].wait()
    loads[1].wait()
    states_of(0, mine, other)
    pl.semaphore_wait(barrier, chips + planes - 1)
    copy0(0).start()
    states_of(0, first, own)
    loads[2].wait()
    loads[3].wait()
    states_of(1, mine, other)
    copy0(1).start()
    chip_sums(0)
    states_of(1, first, own)
    chip_sums(1)

    causal = (lax.broadcasted_iota(jnp.int32, (tokens, tokens), 1)
              <= lax.broadcasted_iota(jnp.int32, (tokens, tokens), 0))

    def within(begin, end):
        for h in range(begin, end):
            cols = slice(h * HEAD_DIM, (h + 1) * HEAD_DIM)
            q, kk, v, g = q_ref[:, cols], k_ref[:, cols], v_ref[:, cols], g_ref[:, cols]
            scores = jnp.where(causal, dot(q, kk, 1, 1), 0.0).astype(jnp.bfloat16)
            dprob = jnp.where(causal, dot(g, v, 1, 1), 0.0).astype(jnp.bfloat16)
            acc[0, :, cols] = dot(scores, v, 1, 0)
            acc[1, :, cols] = dot(dprob, kk, 1, 0)
            acc[2, :, cols] = dot(dprob, q, 0, 0)
            acc[3, :, cols] = dot(scores, g, 0, 0)

    cut1, cut2 = heads * 3 // 8, heads * 5 // 8
    within(0, cut1)

    for a in range(2):
        for k in range(1, chips):
            source = lax.rem(me + chips - k, chips)
            copy1(a, source, source).wait_recv()
        total = got[0, a].astype(jnp.float32)
        for p in range(1, chips):
            total = total + got[p, a].astype(jnp.float32)
        zpart[a] = total.astype(zpart.dtype)
        for zz in range(planes):
            @pl.when(zz > z if a == 0 else zz < z)
            def _():
                copy2(a, zz, z).start()

    for a in range(2):
        for zz in range(planes):
            @pl.when(zz >= z if a == 0 else zz <= z)
            def _():
                zgot[a, zz] = jnp.zeros(zgot.shape[2:], zgot.dtype)

    within(cut1, cut2)

    for a in range(2):
        for zz in range(planes):
            @pl.when(zz < z if a == 0 else zz > z)
            def _():
                copy2(a, zz, zz).wait_recv()
        run = zgot[a, 0].astype(jnp.float32)
        for zz in range(1, planes):
            run = run + zgot[a, zz].astype(jnp.float32)
        order = range(chips) if a == 0 else range(chips - 1, -1, -1)
        for p in order:
            back[p, a] = run.astype(jnp.bfloat16)
            run = run + got[p, a].astype(jnp.float32)
        for k in range(1, chips):
            copy3(a, lax.rem(me + k, chips), me).start()
        chippre[a, rows_of(me), :] = back[me, a]

    within(cut2, heads)

    def finish(start, a):
        for h in range(half):
            cols = cols_of(start + h)
            term = pre[a, cols, :]
            if a == 0:
                o_ref[:, cols] = (acc[0, :, cols] + dot(q_ref[:, cols], term, 1, 0)).astype(jnp.bfloat16)
                gq_ref[:, cols] = (acc[1, :, cols] + dot(g_ref[:, cols], term, 1, 1)).astype(jnp.bfloat16)
            else:
                gk_ref[:, cols] = (acc[2, :, cols] + dot(v_ref[:, cols], term, 1, 1)).astype(jnp.bfloat16)
                gv_ref[:, cols] = (acc[3, :, cols] + dot(k_ref[:, cols], term, 1, 0)).astype(jnp.bfloat16)

    my_rows = pl.ds(pl.multiple_of(core * half_rows, half_rows), half_rows)
    for a in range(2):
        for k in range(1, chips):
            source = lax.rem(me + chips - k, chips)
            copy3(a, source, source).wait_recv()
        base = chippre[a].astype(jnp.float32)
        later = core == (1 if a == 0 else 0)
        mate[a] = (base + jnp.where(later, 0.0, own[a])).astype(jnp.bfloat16)
        copy4(a, core).start()
        pre[a, my_rows, :] = (base + jnp.where(later, paired[a], 0.0)).astype(jnp.bfloat16)
        finish(first, a)
    for a in range(2):
        copy4(a, 1 - core).wait_recv()
        finish(mine, a)

    for a in range(2):
        copy0(a).wait_send()
        copy4(a, core).wait_send()
        for k in range(1, chips):
            there = lax.rem(me + k, chips)
            copy1(a, there, me).wait_send()
            copy3(a, there, me).wait_send()
        for zz in range(planes):
            @pl.when(zz > z if a == 0 else zz < z)
            def _():
                copy2(a, zz, z).wait_send()


def store_kernel(*refs):
    sources, targets, sem = refs[:4], refs[4:8], refs[8]
    copies = [pltpu.make_async_copy(s, t, sem.at[i]) for i, (s, t) in enumerate(zip(sources, targets))]
    for copy in copies:
        copy.start()
    for copy in copies:
        copy.wait()


def per_device(nh, ns, query_rows, key_rows, value_rows, grad_rows):
    tokens, width = query_rows.shape
    nx = 1
    while 2 * (2 * nx) ** 2 <= ns and ns % (2 * nx) == 0:
        nx *= 2
    chips, planes = nh // CORES * nx, ns // nx
    half_rows = width // CORES
    rows = half_rows // chips
    bf16, f32 = jnp.bfloat16, jnp.float32
    vmem, hbm = pl.BlockSpec(memory_space=pltpu.VMEM), pl.BlockSpec(memory_space=pltpu.HBM)
    dma = pltpu.SemaphoreType.DMA
    shape = (jax.ShapeDtypeStruct((tokens, width), bf16),) * 4
    results = pl.pallas_call(
        functools.partial(states_kernel, nh, ns, nx),
        out_shape=shape,
        in_specs=[hbm] * 4,
        out_specs=(vmem,) * 4,
        scratch_shapes=[pltpu.VMEM((tokens, width), bf16)] * 4 + [
            pltpu.VMEM((2, half_rows, HEAD_DIM), f32),
            pltpu.VMEM((2, half_rows, HEAD_DIM), f32),
            pltpu.VMEM((2, half_rows, HEAD_DIM), f32),
            pltpu.VMEM((2, half_rows, HEAD_DIM), bf16),
            pltpu.VMEM((chips, 2, rows, HEAD_DIM), bf16),
            pltpu.VMEM((2, rows, HEAD_DIM), bf16),
            pltpu.VMEM((2, planes, rows, HEAD_DIM), bf16),
            pltpu.VMEM((chips, 2, rows, HEAD_DIM), bf16),
            pltpu.VMEM((2, half_rows, HEAD_DIM), bf16),
            pltpu.VMEM((2, half_rows, HEAD_DIM), bf16),
            pltpu.VMEM((2, width, HEAD_DIM), bf16),
            pltpu.VMEM((4, tokens, width), f32),
            dma((4,)), dma((2,)), dma((2,)), dma((2, chips)), dma((2, chips)),
            dma((2, planes)), dma((2, planes)), dma((2, chips)), dma((2, chips)), dma((2,)), dma((2,)),
        ],
        compiler_params=pltpu.CompilerParams(
            collective_id=0, has_side_effects=True, vmem_limit_bytes=103 * 512 * 1024),
        cost_estimate=pl.CostEstimate(
            flops=tokens * width * (8 * tokens + 12 * HEAD_DIM),
            bytes_accessed=16 * tokens * width, transcendentals=0),
    )(query_rows, key_rows, value_rows, grad_rows)
    return pl.pallas_call(
        store_kernel,
        out_shape=shape,
        in_specs=[vmem] * 4,
        out_specs=(hbm,) * 4,
        scratch_shapes=[dma((4,))],
        compiler_params=pltpu.CompilerParams(vmem_limit_bytes=8 * 1024 * 1024),
        cost_estimate=pl.CostEstimate(flops=0, bytes_accessed=16 * tokens * width, transcendentals=0),
    )(*results)


def solution(mesh):
    placed = P(("seq", "head"), None)
    return jax.shard_map(
        functools.partial(per_device, mesh.shape["head"], mesh.shape["seq"]),
        mesh=mesh,
        in_specs=(placed,) * 4,
        out_specs=(placed,) * 4,
        check_vma=False,
    )
```

```python
import functools

import jax
import jax.numpy as jnp
from jax import lax
from jax.experimental import pallas as pl
from jax.experimental.pallas import tpu as pltpu
from jax.sharding import PartitionSpec as P

HEAD_DIM = 128
CORES = 2
MESH = pl.DeviceIdType.MESH


def dot(a, b, ca, cb):
    return lax.dot_general(a, b, (((ca,), (cb,)), ((), ())), preferred_element_type=jnp.float32)


def states_kernel(nh, ns, nx, q_hbm, k_hbm, v_hbm, g_hbm, o_ref, gq_ref, gk_ref, gv_ref,
                  q_ref, k_ref, v_ref, g_ref, other, paired, own, chip, got, zpart, zgot,
                  back, chippre, mate, pre, acc,
                  in_sem, send0, recv0, send1, recv1, send2, recv2, send3, recv3, send4, recv4):
    tokens, width = q_ref.shape
    heads = width // HEAD_DIM
    half = heads // CORES
    along = nh // CORES
    chips = along * nx
    planes = ns // nx
    half_rows = half * HEAD_DIM
    rows = half_rows // chips
    head_at, seq_at = lax.axis_index("head"), lax.axis_index("seq")
    core = lax.rem(head_at, CORES)
    z = seq_at // nx
    me = lax.rem(seq_at, nx) * along + head_at // CORES
    first, mine = core * half, (1 - core) * half
    partner = {"head": head_at + 1 - 2 * core, "seq": seq_at}

    steps = [(dx, dy) for dx in range(nx) for dy in range(along) if dx or dy]
    steps.sort(key=lambda step: -sum(d > 0 for d in step))
    far_first = [lax.rem(me // along + dx, nx) * along + lax.rem(lax.rem(me, along) + dy, along)
                 for dx, dy in steps]

    def in_plane(p):
        return {"head": lax.rem(p, along) * CORES + core, "seq": z * nx + p // along}

    def in_column(zz):
        return {"head": head_at, "seq": zz * nx + lax.rem(seq_at, nx)}

    def rows_of(p):
        return pl.ds(pl.multiple_of(p * rows, rows), rows)

    def cols_of(h):
        return pl.ds(pl.multiple_of(h * HEAD_DIM, HEAD_DIM), HEAD_DIM)

    loads = [pltpu.make_async_copy(src, dst, in_sem.at[i]) for i, (src, dst) in enumerate(
        ((k_hbm, k_ref), (v_hbm, v_ref), (q_hbm, q_ref), (g_hbm, g_ref)))]
    for load in loads:
        load.start()

    barrier = pltpu.get_barrier_semaphore()
    pl.semaphore_signal(barrier, inc=1, device_id=partner, device_id_type=MESH)
    for k in range(1, chips):
        pl.semaphore_signal(barrier, inc=1, device_id=in_plane(lax.rem(me + k, chips)), device_id_type=MESH)
    for k in range(1, planes):
        pl.semaphore_signal(barrier, inc=1, device_id=in_column(lax.rem(z + k, planes)), device_id_type=MESH)

    def copy0(a):
        return pltpu.make_async_remote_copy(
            src_ref=other.at[a], dst_ref=paired.at[a], send_sem=send0.at[a], recv_sem=recv0.at[a],
            device_id=partner, device_id_type=MESH)

    def copy1(a, there, slot):
        return pltpu.make_async_remote_copy(
            src_ref=chip.at[a, rows_of(there), :], dst_ref=got.at[slot, a],
            send_sem=send1.at[a, there], recv_sem=recv1.at[a, slot],
            device_id=in_plane(there), device_id_type=MESH)

    def copy2(a, zz, slot):
        return pltpu.make_async_remote_copy(
            src_ref=zpart.at[a], dst_ref=zgot.at[a, slot],
            send_sem=send2.at[a, zz], recv_sem=recv2.at[a, slot],
            device_id=in_column(zz), device_id_type=MESH)

    def copy3(a, there, owner):
        return pltpu.make_async_remote_copy(
            src_ref=back.at[there, a], dst_ref=chippre.at[a, rows_of(owner), :],
            send_sem=send3.at[a, there], recv_sem=recv3.at[a, owner],
            device_id=in_plane(there), device_id_type=MESH)

    def copy4(a, whose):
        return pltpu.make_async_remote_copy(
            src_ref=mate.at[a],
            dst_ref=pre.at[a, pl.ds(pl.multiple_of(whose * half_rows, half_rows), half_rows), :],
            send_sem=send4.at[a], recv_sem=recv4.at[a], device_id=partner, device_id_type=MESH)

    def states_of(a, start, out):
        x_ref, y_ref = ((k_ref, v_ref), (q_ref, g_ref))[a]
        for h in range(half):
            cols, at = cols_of(start + h), slice(h * HEAD_DIM, (h + 1) * HEAD_DIM)
            out[a, at, :] = dot(x_ref[:, cols], y_ref[:, cols], 0, 0)

    def chip_sums(a):
        copy0(a).wait_recv()
        chip[a] = (own[a] + paired[a]).astype(chip.dtype)
        for there in far_first:
            copy1(a, there, me).start()
        got[me, a] = chip[a, rows_of(me), :]

    loads[0].wait()
    loads[1].wait()
    states_of(0, mine, other)
    pl.semaphore_wait(barrier, chips + planes - 1)
    copy0(0).start()
    states_of(0, first, own)
    loads[2].wait()
    loads[3].wait()
    states_of(1, mine, other)
    copy0(1).start()
    chip_sums(0)
    states_of(1, first, own)
    chip_sums(1)

    causal = (lax.broadcasted_iota(jnp.int32, (tokens, tokens), 1)
              <= lax.broadcasted_iota(jnp.int32, (tokens, tokens), 0))

    def within(begin, end):
        for h in range(begin, end):
            cols = slice(h * HEAD_DIM, (h + 1) * HEAD_DIM)
            q, kk, v, g = q_ref[:, cols], k_ref[:, cols], v_ref[:, cols], g_ref[:, cols]
            scores = jnp.where(causal, dot(q, kk, 1, 1), 0.0).astype(jnp.bfloat16)
            dprob = jnp.where(causal, dot(g, v, 1, 1), 0.0).astype(jnp.bfloat16)
            acc[0, :, cols] = dot(scores, v, 1, 0)
            acc[1, :, cols] = dot(dprob, kk, 1, 0)
            acc[2, :, cols] = dot(dprob, q, 0, 0)
            acc[3, :, cols] = dot(scores, g, 0, 0)

    cut1, cut2 = heads * 3 // 8, heads * 5 // 8
    within(0, cut1)

    for a in range(2):
        for k in range(1, chips):
            source = lax.rem(me + chips - k, chips)
            copy1(a, source, source).wait_recv()
        total = got[0, a].astype(jnp.float32)
        for p in range(1, chips):
            total = total + got[p, a].astype(jnp.float32)
        zpart[a] = total.astype(zpart.dtype)
        for zz in range(planes):
            @pl.when(zz > z if a == 0 else zz < z)
            def _():
                copy2(a, zz, z).start()

    for a in range(2):
        for zz in range(planes):
            @pl.when(zz >= z if a == 0 else zz <= z)
            def _():
                zgot[a, zz] = jnp.zeros(zgot.shape[2:], zgot.dtype)

    within(cut1, cut2)

    for a in range(2):
        for zz in range(planes):
            @pl.when(zz < z if a == 0 else zz > z)
            def _():
                copy2(a, zz, zz).wait_recv()
        run = zgot[a, 0].astype(jnp.float32)
        for zz in range(1, planes):
            run = run + zgot[a, zz].astype(jnp.float32)
        order = range(chips) if a == 0 else range(chips - 1, -1, -1)
        for p in order:
            back[p, a] = run.astype(jnp.bfloat16)
            run = run + got[p, a].astype(jnp.float32)
        for there in far_first:
            copy3(a, there, me).start()
        chippre[a, rows_of(me), :] = back[me, a]

    within(cut2, heads)

    def finish(start, a):
        for h in range(half):
            cols = cols_of(start + h)
            term = pre[a, cols, :]
            if a == 0:
                o_ref[:, cols] = (acc[0, :, cols] + dot(q_ref[:, cols], term, 1, 0)).astype(jnp.bfloat16)
                gq_ref[:, cols] = (acc[1, :, cols] + dot(g_ref[:, cols], term, 1, 1)).astype(jnp.bfloat16)
            else:
                gk_ref[:, cols] = (acc[2, :, cols] + dot(v_ref[:, cols], term, 1, 1)).astype(jnp.bfloat16)
                gv_ref[:, cols] = (acc[3, :, cols] + dot(k_ref[:, cols], term, 1, 0)).astype(jnp.bfloat16)

    my_rows = pl.ds(pl.multiple_of(core * half_rows, half_rows), half_rows)
    for a in range(2):
        for k in range(1, chips):
            source = lax.rem(me + chips - k, chips)
            copy3(a, source, source).wait_recv()
        base = chippre[a].astype(jnp.float32)
        later = core == (1 if a == 0 else 0)
        mate[a] = (base + jnp.where(later, 0.0, own[a])).astype(jnp.bfloat16)
        copy4(a, core).start()
        pre[a, my_rows, :] = (base + jnp.where(later, paired[a], 0.0)).astype(jnp.bfloat16)
        finish(first, a)
    for a in range(2):
        copy4(a, 1 - core).wait_recv()
        finish(mine, a)

    for a in range(2):
        copy0(a).wait_send()
        copy4(a, core).wait_send()
        for k in range(1, chips):
            there = lax.rem(me + k, chips)
            copy1(a, there, me).wait_send()
            copy3(a, there, me).wait_send()
        for zz in range(planes):
            @pl.when(zz > z if a == 0 else zz < z)
            def _():
                copy2(a, zz, z).wait_send()


def store_kernel(*refs):
    sources, targets, sem = refs[:4], refs[4:8], refs[8]
    copies = [pltpu.make_async_copy(s, t, sem.at[i]) for i, (s, t) in enumerate(zip(sources, targets))]
    for copy in copies:
        copy.start()
    for copy in copies:
        copy.wait()


def per_device(nh, ns, query_rows, key_rows, value_rows, grad_rows):
    tokens, width = query_rows.shape
    nx = 1
    while 2 * (2 * nx) ** 2 <= ns and ns % (2 * nx) == 0:
        nx *= 2
    chips, planes = nh // CORES * nx, ns // nx
    half_rows = width // CORES
    rows = half_rows // chips
    bf16, f32 = jnp.bfloat16, jnp.float32
    vmem, hbm = pl.BlockSpec(memory_space=pltpu.VMEM), pl.BlockSpec(memory_space=pltpu.HBM)
    dma = pltpu.SemaphoreType.DMA
    shape = (jax.ShapeDtypeStruct((tokens, width), bf16),) * 4
    results = pl.pallas_call(
        functools.partial(states_kernel, nh, ns, nx),
        out_shape=shape,
        in_specs=[hbm] * 4,
        out_specs=(vmem,) * 4,
        scratch_shapes=[pltpu.VMEM((tokens, width), bf16)] * 4 + [
            pltpu.VMEM((2, half_rows, HEAD_DIM), f32),
            pltpu.VMEM((2, half_rows, HEAD_DIM), f32),
            pltpu.VMEM((2, half_rows, HEAD_DIM), f32),
            pltpu.VMEM((2, half_rows, HEAD_DIM), bf16),
            pltpu.VMEM((chips, 2, rows, HEAD_DIM), bf16),
            pltpu.VMEM((2, rows, HEAD_DIM), bf16),
            pltpu.VMEM((2, planes, rows, HEAD_DIM), bf16),
            pltpu.VMEM((chips, 2, rows, HEAD_DIM), bf16),
            pltpu.VMEM((2, half_rows, HEAD_DIM), bf16),
            pltpu.VMEM((2, half_rows, HEAD_DIM), bf16),
            pltpu.VMEM((2, width, HEAD_DIM), bf16),
            pltpu.VMEM((4, tokens, width), f32),
            dma((4,)), dma((2,)), dma((2,)), dma((2, chips)), dma((2, chips)),
            dma((2, planes)), dma((2, planes)), dma((2, chips)), dma((2, chips)), dma((2,)), dma((2,)),
        ],
        compiler_params=pltpu.CompilerParams(
            collective_id=0, has_side_effects=True, vmem_limit_bytes=103 * 512 * 1024),
        cost_estimate=pl.CostEstimate(
            flops=tokens * width * (8 * tokens + 12 * HEAD_DIM),
            bytes_accessed=16 * tokens * width, transcendentals=0),
    )(query_rows, key_rows, value_rows, grad_rows)
    return pl.pallas_call(
        store_kernel,
        out_shape=shape,
        in_specs=[vmem] * 4,
        out_specs=(hbm,) * 4,
        scratch_shapes=[dma((4,))],
        compiler_params=pltpu.CompilerParams(vmem_limit_bytes=8 * 1024 * 1024),
        cost_estimate=pl.CostEstimate(flops=0, bytes_accessed=16 * tokens * width, transcendentals=0),
    )(*results)


def solution(mesh):
    placed = P(("seq", "head"), None)
    return jax.shard_map(
        functools.partial(per_device, mesh.shape["head"], mesh.shape["seq"]),
        mesh=mesh,
        in_specs=(placed,) * 4,
        out_specs=(placed,) * 4,
        check_vma=False,
    )
```
